32 devices in a mesh: rows: 32 (over z, y, x, core).
Axes of the slice: x: 2, y: 2, z: 4, core: 2. Of those that a mesh axis runs over, the one named last changes fastest.
Arguments:
- features: float32 [16384, 256], P('rows'), may hold values from -6 to 6
- adjacency: float32 [64, 6, 256, 256], P('rows'), may hold values from -0.25 to 0.25
- block_index: int32 [64, 6], P('rows'), may hold values from 0 to 63, as said below
- block_counts: int32 [64], P('rows'), may hold values from 1 to 6, as said below
- labels: int32 [16384], P('rows'), may hold values from 0 to 127
- weight_in: float32 [256, 512], replicated, may hold values from -0.375 to 0.375
- weight_out: float32 [512, 128], replicated, may hold values from -0.25 to 0.25
Outputs:
- logits: float32 [16384, 128], P('rows')
- mean_loss: float32 [], replicated
- hidden_grad: float32 [16384, 512], P('rows')
- grad_in: float32 [256, 512], replicated
- grad_out: float32 [512, 128], replicated
The draws below stay inside these ranges and needn't reach their ends.
Inputs may be any that keep to these rules, and one draw needn't show every extreme that they name: `block_index`: row block b lies on device b // 2; every slot's column block lies at most 2 row blocks away from b, inside the graph. `block_counts`: some row block uses all 6 slots.
All inputs are finite; a program needn't handle non-finite values.
Results may differ from the reference program's by a relative error of at most 0.00011.
Values sent between devices are 32-bit elements; how exact they have to be, the bound alone decides.
A program may use at most 64 MiB of HBM per device.

```python
import jax
import jax.numpy as jnp
from jax import lax

BLOCK = 256
F_IN = 256
HID = 512
CLASSES = 128
SLOTS = 6
REACH = 2
BLOCKS = 64
NODES = 16384


def draw_block_index(key, part):
    key = jax.random.fold_in(key, 11)
    block_ids = jnp.arange(BLOCKS, dtype=jnp.int32)
    lowest = jnp.maximum(block_ids - REACH, 0)
    highest = jnp.minimum(block_ids + REACH + 1, BLOCKS)
    raw = jax.random.randint(key, (BLOCKS, SLOTS), 0, 1073741824, dtype=jnp.int32)
    return (lowest[:, None] + raw % (highest - lowest)[:, None]).astype(jnp.int32)


def draw_block_counts(key, part):
    key = jax.random.fold_in(key, 12)
    first, third = jax.random.split(key, 2)
    counts = 1 + jax.random.randint(first, (BLOCKS,), 0, SLOTS, dtype=jnp.int32)
    fullest = jax.random.randint(third, (), 0, BLOCKS, dtype=jnp.int32)
    counts = jnp.where(jnp.arange(BLOCKS, dtype=jnp.int32) == fullest, SLOTS, counts)
    return counts.astype(jnp.int32)


def place_ends(drawn, stream_key, least, high):
    place = [jax.random.randint(jax.random.fold_in(stream_key, axis), (), 0, length) for axis, length in enumerate(drawn.shape)]
    widest = drawn.shape.index(max(drawn.shape))
    next_to = place[:widest] + [(place[widest] + 1) % drawn.shape[widest]] + place[widest + 1:]
    return drawn.at[tuple(place)].set(least).at[tuple(next_to)].set(high)


def shard_levels(own_key, dims, shards, smallest, high):
    def one(position, parts):
        steps = jax.random.uniform(jax.random.fold_in(jax.random.fold_in(own_key, 6), position), (parts,), jnp.float32, smallest / len(shards), high / len(shards))
        return jnp.repeat(jnp.exp(steps), dims[position] // parts).reshape((-1,) + (1,) * (len(dims) - position - 1))

    gain = one(*shards[0])
    for cut in shards[1:]:
        gain = gain * one(*cut)
    return gain


def noise(own_key, dims, scale, limit, shards=(), kind=jnp.bfloat16):
    values = jax.random.normal(own_key, dims, jnp.float32) * scale
    if len(shards) > 0:
        values = shard_levels(own_key, dims, shards, -0.22, 0.18) * values
    return jnp.clip(values, min=-limit, max=limit).astype(kind)


def setup_inputs(seed: int = 0) -> dict:
    keys = jax.random.split(jax.random.key(seed), 8)
    return {
        "features": noise(keys[0], (NODES, F_IN), 1.0, 6.0, ((0, 32),), jnp.float32),
        "adjacency": noise(keys[1], (BLOCKS, SLOTS, BLOCK, BLOCK), (2 * BLOCK) ** -0.5, 0.25, ((0, 32),), jnp.float32),
        "block_index": draw_block_index(jax.random.fold_in(keys[7], 71), 0),
        "block_counts": draw_block_counts(jax.random.fold_in(keys[7], 71), 0),
        "labels": place_ends(jax.random.randint(keys[4], (NODES,), 0, CLASSES), jax.random.fold_in(keys[4], 1), 0, CLASSES - 1).astype(jnp.int32),
        "weight_in": noise(keys[5], (F_IN, HID), F_IN ** -0.5, 0.375, (), jnp.float32),
        "weight_out": noise(keys[6], (HID, CLASSES), HID ** -0.5, 0.25, (), jnp.float32),
    }


HIGH = lax.Precision.HIGHEST

def activate(values):
    return jax.nn.gelu(values, approximate=False)

def propagate(values, adjacency, block_index, block_counts):
    block_rows = adjacency.shape[2]
    grouped = values.reshape(adjacency.shape[0], block_rows, values.shape[1])
    usable_all = jnp.arange(adjacency.shape[1], dtype=jnp.int32)[None, :] < block_counts[:, None]

    def one_block(packed):
        tiles, column_ids, usable = packed
        picked = grouped[column_ids]
        tiles = jnp.where(usable[:, None, None], tiles, jnp.zeros_like(tiles))
        return jnp.einsum('kij,kjw->iw', tiles, picked, precision=HIGH)
    result = lax.map(one_block, (adjacency, block_index, usable_all))
    return result.reshape(-1, values.shape[1])

def reference(features, adjacency, block_index, block_counts, labels, weight_in, weight_out):
    spread_in = propagate(features, adjacency, block_index, block_counts)
    pre_hidden = jnp.dot(spread_in, weight_in, precision=HIGH)
    hidden = activate(pre_hidden)
    spread_hidden = propagate(hidden, adjacency, block_index, block_counts)
    logits = jnp.dot(spread_hidden, weight_out, precision=HIGH)
    totals = jnp.log(lax.optimization_barrier(jnp.sum(jnp.exp(logits), axis=1)))
    onehot = (labels[:, None] == jnp.arange(CLASSES, dtype=jnp.int32)[None, :]).astype(logits.dtype)
    row_loss = totals - lax.optimization_barrier(jnp.sum(onehot * logits, axis=1))
    mean_loss = jnp.sum(row_loss) / NODES
    logit_grad = jnp.exp(logits - totals[:, None]) - onehot
    grad_out = jnp.dot(spread_hidden.T, logit_grad, precision=HIGH)
    _, pull = jax.vjp(lambda values: propagate(values, adjacency, block_index, block_counts), jnp.zeros_like(logit_grad))
    returned = pull(logit_grad)[0]
    hidden_grad = jnp.dot(returned, weight_out.T, precision=HIGH)
    _, back = jax.vjp(activate, pre_hidden)
    pre_grad = back(hidden_grad)[0]
    grad_in = jnp.dot(spread_in.T, pre_grad, precision=HIGH)
    return (logits, mean_loss, hidden_grad, grad_in, grad_out)
```

```python
import functools

import jax
import jax.numpy as jnp
from jax import lax
from jax.experimental import pallas as pl
from jax.experimental.pallas import tpu as pltpu
from jax.sharding import PartitionSpec as P

REACH = 2
F32 = jnp.float32
BF16 = jnp.bfloat16
MESH = pl.DeviceIdType.MESH
PARTS = 3
SMALLEST = 16


def split(value):
    high = value.astype(BF16)
    return high, (value - high.astype(F32)).astype(BF16)


def mm(a_high, a_low, b_high, b_low):
    def one(a, b):
        return jnp.dot(a, b, preferred_element_type=F32)

    return one(a_high, b_high) + (one(a_high, b_low) + one(a_low, b_high))


def chunks(total, size, body):
    def step(i, carry):
        body(pl.ds(pl.multiple_of(i * size, size), size))
        return carry

    lax.fori_loop(0, total // size, step, 0)


def plan(n, rows):
    bits = list(range(n.bit_length() - 1))
    parts = []
    for part in range(PARTS):
        near = bits[1:4]
        turn = part % max(1, len(near))
        order = bits[:1] + near[turn:] + near[:turn] + bits[4:]
        length, offset, steps = rows, 0, []
        for bit in order:
            halves = length > SMALLEST
            if halves:
                length //= 2
            steps.append((bit, length, offset, halves))
            offset += length
        parts.append(steps)
    return parts, offset


def kernel(
    n, steps, index_ref, counts_ref, features, adjacency, labels, weight_in, weight_out,
    logits_ref, loss_ref, hidden_grad_ref, grad_in_ref, grad_out_ref,
    far_features, band, band_high, band_low, turned_high, turned_low,
    near_high, near_low, win_high, win_low, wout_high, wout_low, back_high, back_low,
    spread_high, spread_low, spread_t_high, spread_t_low, spread, hidden, slope, hid_high, hid_low, hid_t_high, hid_t_low,
    near_z, z_high, z_low, grad_high, grad_low, out_low, out_high, in_low, in_high, returned,
    acc, landing, full, loss_acc, loss_in,
    halo_send, halo_recv, part_send, part_recv, loss_send, loss_recv,
):
    me = lax.axis_index("rows")
    own = features.shape[0]
    block = adjacency.shape[2]
    here, slots = adjacency.shape[0], adjacency.shape[1]
    wide = 2 * REACH + 1
    hid = weight_in.shape[1]
    classes = weight_out.shape[1]
    has_low, has_high = me > 0, me < n - 1
    lower, upper = jnp.maximum(me - 1, 0), jnp.minimum(me + 1, n - 1)
    bits = n.bit_length() - 1

    barrier = pltpu.get_barrier_semaphore()
    for bit in range(bits):
        other = me + (1 << bit) - 2 * (1 << bit) * lax.rem(lax.div(me, 1 << bit), 2)
        pl.semaphore_signal(barrier, inc=1, device_id=(other,), device_id_type=MESH)

    @pl.when(has_low)
    def _():
        pl.semaphore_signal(barrier, inc=1, device_id=(lower,), device_id_type=MESH)

    @pl.when(has_high)
    def _():
        pl.semaphore_signal(barrier, inc=1, device_id=(upper,), device_id_type=MESH)

    pl.semaphore_wait(barrier, bits + jnp.where(has_low, 1, 0) + jnp.where(has_high, 1, 0))

    def exchange(slot, to_upper, at_upper, to_lower, at_lower):
        up = pltpu.make_async_remote_copy(
            src_ref=to_upper, dst_ref=at_upper, send_sem=halo_send.at[slot, 0], recv_sem=halo_recv.at[slot, 0],
            device_id=(upper,), device_id_type=MESH)
        down = pltpu.make_async_remote_copy(
            src_ref=to_lower, dst_ref=at_lower, send_sem=halo_send.at[slot, 1], recv_sem=halo_recv.at[slot, 1],
            device_id=(lower,), device_id_type=MESH)

        def start_up():
            @pl.when(has_high)
            def _():
                up.start()

        def start_down():
            @pl.when(has_low)
            def _():
                down.start()

        def finish():
            @pl.when(has_high)
            def _():
                up.wait_send()
                down.wait_recv()

            @pl.when(has_low)
            def _():
                down.wait_send()
                up.wait_recv()

            @pl.when(jnp.logical_not(has_low))
            def _():
                at_upper[...] = jnp.zeros(at_upper.shape, F32)

            @pl.when(jnp.logical_not(has_high))
            def _():
                at_lower[...] = jnp.zeros(at_lower.shape, F32)

        return start_up, start_down, finish

    start_up, start_down, finish_features = exchange(
        0, features, far_features.at[0], features, far_features.at[1])
    start_up()
    start_down()

    for b in range(here):
        weights = []
        for k in range(slots):
            relative = index_ref[b, k] - (me * here - REACH) - b
            used = k < counts_ref[b]
            weights.append([
                jnp.where(jnp.logical_and(used, relative == j), 1.0, 0.0).astype(F32) for j in range(wide)])

        def densify(rows, b=b, weights=weights):
            sums = [None] * wide
            for k in range(slots):
                tile = adjacency[b, k, rows, :]
                for j in range(wide):
                    term = weights[k][j] * tile
                    sums[j] = term if k == 0 else sums[j] + term
            for j in range(wide):
                columns = slice(j * block, (j + 1) * block)
                high, low = split(sums[j])
                band[b, rows, columns] = sums[j]
                band_high[b, rows, columns] = high
                band_low[b, rows, columns] = low

        chunks(block, 32, densify)
        for j in range(wide):
            columns = slice(j * block, (j + 1) * block)
            high, low = split(band[b, :, columns].T)
            turned_high[b, columns, :] = high
            turned_low[b, columns, :] = low
    win_high[...], win_low[...] = split(weight_in[...])
    wout_high[...], wout_low[...] = split(weight_out[...])
    back_high[...], back_low[...] = split(weight_out[...].T)
    middle = slice(own, 2 * own)
    near_high[middle, :], near_low[middle, :] = split(features[...])
    finish_features()
    for side, start in ((0, 0), (1, 2 * own)):
        rows = slice(start, start + own)
        near_high[rows, :], near_low[rows, :] = split(far_features[side])

    for b in range(here):
        rows = slice(b * block, (b + 1) * block)
        cols = slice(b * block, (b + wide) * block)
        value = mm(band_high[b], band_low[b], near_high[cols, :], near_low[cols, :])
        spread[rows, :] = value
        spread_high[rows, :], spread_low[rows, :] = split(value)

    slope[...] = mm(spread_high[...], spread_low[...], win_high[...], win_low[...])

    def gelu(rows):
        x = slope[rows, :]
        below = 0.5 * (1.0 + lax.erf(x * 0.7071067811865476))
        value = x * below
        hidden[rows, :] = value
        hid_high[rows, :], hid_low[rows, :] = split(value)
        slope[rows, :] = below + x * (jnp.exp(-0.5 * x * x) * 0.3989422804014327)

    chunks(own, 32, gelu)
    near_z[middle, :] = mm(hid_high[...], hid_low[...], wout_high[...], wout_low[...])

    start_up, start_down, finish_z = exchange(
        1, near_z.at[pl.ds(own, own)], near_z.at[pl.ds(0, own)],
        near_z.at[pl.ds(own, own)], near_z.at[pl.ds(2 * own, own)])
    start_up()
    start_down()
    for b in range(here):
        rows = slice(b * block, (b + 1) * block)
        spread_t_high[:, rows], spread_t_low[:, rows] = split(spread[rows, :].T)
        for c in range(hid // block):
            columns = slice(c * block, (c + 1) * block)
            hid_t_high[columns, rows], hid_t_low[columns, rows] = split(hidden[rows, columns].T)
    finish_z()
    z_high[...], z_low[...] = split(near_z[...])

    loss_acc[...] = jnp.zeros(loss_acc.shape, F32)
    for b in range(here):
        rows = slice(b * block, (b + 1) * block)
        cols = slice(b * block, (b + wide) * block)
        logits = mm(band_high[b], band_low[b], z_high[cols, :], z_low[cols, :])
        logits_ref[rows, :] = logits
        totals = jnp.log(jnp.sum(jnp.exp(logits), axis=1, keepdims=True))
        lanes = lax.broadcasted_iota(jnp.int32, logits.shape, 1)
        onehot = jnp.where(labels[rows, :] == lanes, 1.0, 0.0).astype(F32)
        row_loss = totals - jnp.sum(onehot * logits, axis=1, keepdims=True)
        loss_acc[...] += jnp.broadcast_to(jnp.sum(row_loss, axis=0, keepdims=True), loss_acc.shape)
        grad_high[rows, :], grad_low[rows, :] = split(jnp.exp(logits - totals) - onehot)

    def bucket(start):
        pieces = []
        for j in range(start // block, (start + own) // block):
            total = None
            for b in range(here):
                if 0 <= j - b < wide:
                    columns = slice((j - b) * block, (j - b + 1) * block)
                    rows = slice(b * block, (b + 1) * block)
                    term = mm(turned_high[b, columns, :], turned_low[b, columns, :], grad_high[rows, :], grad_low[rows, :])
                    total = term if total is None else total + term
            pieces.append(total)
        return pieces

    start_up, start_down, finish_returned = exchange(2, out_high, in_low, out_low, in_high)
    for i, piece in enumerate(bucket(2 * own)):
        out_high[i * block : (i + 1) * block, :] = piece
    start_up()
    for i, piece in enumerate(bucket(0)):
        out_low[i * block : (i + 1) * block, :] = piece
    start_down()
    for i, piece in enumerate(bucket(own)):
        returned[i * block : (i + 1) * block, :] = piece
    finish_returned()
    returned[...] = returned[...] + (in_low[...] + in_high[...])
    grad_high[...], grad_low[...] = split(returned[...])

    lows = [0] * PARTS

    def partner_of(bit):
        mine = lax.rem(lax.div(me, 1 << bit), 2)
        return mine, me + (1 << bit) - 2 * (1 << bit) * mine

    def start_step(part, s):
        bit, length, offset, halves = steps[part][s]
        mine, other = partner_of(bit)
        low = lows[part]
        source = low + (1 - mine) * length if halves else low
        copy = pltpu.make_async_remote_copy(
            src_ref=acc.at[part, pl.ds(pl.multiple_of(source, SMALLEST), length)],
            dst_ref=landing.at[part, pl.ds(offset, length)],
            send_sem=part_send.at[0, part, s], recv_sem=part_recv.at[0, part, s],
            device_id=(other,), device_id_type=MESH)
        copy.start()
        if halves:
            lows[part] = low + mine * length
        return copy

    def finish_step(part, s, copy):
        _, length, offset, _ = steps[part][s]
        copy.wait()
        rows = pl.ds(pl.multiple_of(lows[part], SMALLEST), length)
        acc[part, rows, :] = acc[part, rows, :] + landing[part, pl.ds(offset, length), :]

    def start_loss(s):
        _, other = partner_of(steps[0][s][0])
        copy = pltpu.make_async_remote_copy(
            src_ref=loss_acc, dst_ref=loss_in.at[s], send_sem=loss_send.at[s], recv_sem=loss_recv.at[s],
            device_id=(other,), device_id_type=MESH)
        copy.start()
        return copy

    acc[2] = mm(hid_t_high[...], hid_t_low[...], grad_high[...], grad_low[...])
    last_copy = start_step(2, 0)
    loss_copy = start_loss(0)
    hidden_grad_ref[...] = mm(grad_high[...], grad_low[...], back_high[...], back_low[...])

    def pre_grad(rows):
        hid_high[rows, :], hid_low[rows, :] = split(hidden_grad_ref[rows, :] * slope[rows, :])

    chunks(own, 32, pre_grad)
    first = []
    for part in range(2):
        columns = slice(part * hid // 2, (part + 1) * hid // 2)
        value = mm(spread_t_high[...], spread_t_low[...], hid_high[:, columns], hid_low[:, columns])
        for i in range(2):
            acc[part, i * block : (i + 1) * block, :] = value[:, i * classes : (i + 1) * classes]
        first.append(start_step(part, 0))
    copies = first + [last_copy]
    for s in range(bits):
        if s > 0:
            loss_copy = start_loss(s)
            copies = [start_step(part, s) for part in range(PARTS)]
        for part in range(PARTS):
            finish_step(part, s, copies[part])
        loss_copy.wait()
        loss_acc[...] = loss_acc[...] + loss_in[s]
    loss_ref[...] = loss_acc[...]

    for part in range(PARTS):
        rows = pl.ds(pl.multiple_of(lows[part], SMALLEST), steps[part][-1][1])
        full[part, rows, :] = acc[part, rows, :]
    for s in reversed(range(bits)):
        copies = []
        for part in range(PARTS):
            bit, length, _, halves = steps[part][s]
            if not halves:
                continue
            mine, other = partner_of(bit)
            rows = pl.ds(pl.multiple_of(lows[part], SMALLEST), length)
            copy = pltpu.make_async_remote_copy(
                src_ref=full.at[part, rows], dst_ref=full.at[part, rows],
                send_sem=part_send.at[1, part, s], recv_sem=part_recv.at[1, part, s],
                device_id=(other,), device_id_type=MESH)
            copy.start()
            copies.append(copy)
            lows[part] = lows[part] - mine * length
        for copy in copies:
            copy.wait()
    for part in range(2):
        for i in range(2):
            columns = slice((2 * part + i) * classes, (2 * part + i + 1) * classes)
            grad_in_ref[:, columns] = full[part, i * block : (i + 1) * block, :]
    grad_out_ref[...] = full[2]


def per_device(n, features, adjacency, block_index, block_counts, labels, weight_in, weight_out):
    own, f_in = features.shape
    here, _, block, _ = adjacency.shape
    hid, classes = weight_out.shape
    wide = 2 * REACH + 1
    rows = hid
    steps, landing = plan(n, rows)
    bits = n.bit_length() - 1

    def both(*shape):
        return [pltpu.VMEM(shape, BF16)] * 2

    def plain(*shape):
        return pltpu.VMEM(shape, F32)

    scratch = [
        plain(2, own, f_in), plain(here, block, wide * block), *both(here, block, wide * block),
        *both(here, wide * block, block), *both(3 * own, f_in), *both(f_in, hid), *both(hid, classes),
        *both(classes, hid), *both(own, f_in), *both(f_in, own), plain(own, f_in), plain(own, hid), plain(own, hid),
        *both(own, hid), *both(hid, own), plain(3 * own, classes), *both(3 * own, classes), *both(own, classes),
        plain(own, classes), plain(own, classes), plain(own, classes), plain(own, classes), plain(own, classes),
        plain(PARTS, rows, classes), plain(PARTS, landing, classes), plain(PARTS, rows, classes),
        plain(8, 128), plain(bits, 8, 128),
        pltpu.SemaphoreType.DMA((3, 2)), pltpu.SemaphoreType.DMA((3, 2)),
        pltpu.SemaphoreType.DMA((2, PARTS, bits)), pltpu.SemaphoreType.DMA((2, PARTS, bits)),
        pltpu.SemaphoreType.DMA((bits,)), pltpu.SemaphoreType.DMA((bits,)),
    ]
    shapes = [(own, classes), (8, 128), (own, hid), (f_in, hid), (hid, classes)]
    logits, loss, hidden_grad, grad_in, grad_out = pl.pallas_call(
        functools.partial(kernel, n, steps),
        out_shape=[jax.ShapeDtypeStruct(shape, F32) for shape in shapes],
        in_specs=[pl.BlockSpec(memory_space=pltpu.SMEM)] * 2 + [pl.BlockSpec(memory_space=pltpu.VMEM)] * 5,
        out_specs=[pl.BlockSpec(memory_space=pltpu.VMEM)] * 5,
        scratch_shapes=scratch,
        compiler_params=pltpu.CompilerParams(
            collective_id=0, has_side_effects=True, vmem_limit_bytes=56 * 1024 * 1024),
        name="step",
    )(block_index, block_counts, features, adjacency, labels[:, None], weight_in, weight_out)
    return (logits, loss[0, 0] / (own * n), hidden_grad, grad_in, grad_out)


def solution(mesh):
    in_specs = (
        P("rows", None),
        P("rows", None, None, None),
        P("rows", None),
        P("rows"),
        P("rows"),
        P(),
        P(),
    )
    out_specs = (P("rows", None), P(), P("rows", None), P(), P())
    return jax.shard_map(
        functools.partial(per_device, mesh.shape["rows"]),
        mesh=mesh, in_specs=in_specs, out_specs=out_specs, check_vma=False,
    )
```

```python
import functools

import jax
import jax.numpy as jnp
from jax import lax
from jax.experimental import pallas as pl
from jax.experimental.pallas import tpu as pltpu
from jax.sharding import PartitionSpec as P

REACH = 2
F32 = jnp.float32
BF16 = jnp.bfloat16
MESH = pl.DeviceIdType.MESH
PARTS = 3
SMALLEST = 16


def split(value):
    high = value.astype(BF16)
    return high, (value - high.astype(F32)).astype(BF16)


def mm(a_high, a_low, b_high, b_low):
    def one(a, b):
        return jnp.dot(a, b, preferred_element_type=F32)

    return one(a_high, b_high) + (one(a_high, b_low) + one(a_low, b_high))


def chunks(total, size, body):
    def step(i, carry):
        body(pl.ds(pl.multiple_of(i * size, size), size))
        return carry

    lax.fori_loop(0, total // size, step, 0)


def plan(n, rows):
    bits = list(range(n.bit_length() - 1))
    cut = min(len(bits), (rows // SMALLEST).bit_length() - 1)
    parts = []
    for part in range(PARTS):
        near = bits[1:4]
        turn = part % max(1, len(near))
        order = bits[:1] + near[turn:] + near[:turn] + bits[4:]
        groups = [(bit,) for bit in order[: cut - 2]] + [tuple(order[cut - 2 : cut])] + [(bit,) for bit in order[cut:]]
        length, offset, message, steps = rows, 0, 0, []
        for number, group in enumerate(groups):
            members = 1 << len(group)
            cuts = number < cut - 1
            if cuts:
                length //= members
            steps.append((group, length, offset, message, cuts))
            offset += (members - 1) * length
            message += members - 1
        parts.append(steps)
    return parts, offset, message


def kernel(
    n, steps, index_ref, counts_ref, features, adjacency_hbm, labels, weight_in, weight_out,
    logits_out, loss_out, hidden_grad_out, packed_out,
    adjacency, far_features, band, band_high, band_low, turned_high, turned_low,
    near_high, near_low, win_high, win_low, wout_high, wout_low, back_high, back_low,
    spread_high, spread_low, spread_t_high, spread_t_low, spread, hidden, slope, hid_high, hid_low, hid_t_high, hid_t_low,
    onehot_ref, near_z, z_high, z_low, logits_ref, grad_high, grad_low, out_low, out_high, in_low, in_high, returned,
    ret_high, ret_low, hidden_grad, acc, landing, full, loss_acc, loss_in,
    halo_send, halo_recv, part_send, part_recv, loss_send, loss_recv, local_sem,
):
    me = lax.axis_index("rows")
    own = features.shape[0]
    here, slots, block = adjacency.shape[:3]
    wide = 2 * REACH + 1
    hid = weight_in.shape[1]
    classes = weight_out.shape[1]
    has_low, has_high = me > 0, me < n - 1
    lower, upper = jnp.maximum(me - 1, 0), jnp.minimum(me + 1, n - 1)

    fetch = pltpu.make_async_copy(adjacency_hbm, adjacency, local_sem.at[0])
    fetch.start()

    def bit_of(bit):
        return lax.rem(lax.div(me, 1 << bit), 2)

    def member(group, delta):
        other, theirs, mine = me, 0, 0
        for position, bit in enumerate(group):
            weight = 1 << (len(group) - 1 - position)
            value = bit_of(bit)
            mine = mine + value * weight
            if delta & weight:
                other = other + (1 - 2 * value) * (1 << bit)
                theirs = theirs + (1 - value) * weight
            else:
                theirs = theirs + value * weight
        return other, theirs, mine

    partners = sorted({
        sum(1 << bit for position, bit in enumerate(step[0]) if delta & (1 << (len(step[0]) - 1 - position)))
        for part in steps for step in part for delta in range(1, 1 << len(step[0]))})
    barrier = pltpu.get_barrier_semaphore()
    for mask in partners:
        other = me
        for bit in range(n.bit_length() - 1):
            if mask >> bit & 1:
                other = other + (1 - 2 * bit_of(bit)) * (1 << bit)
        pl.semaphore_signal(barrier, inc=1, device_id=(other,), device_id_type=MESH)

    @pl.when(has_low)
    def _():
        pl.semaphore_signal(barrier, inc=1, device_id=(lower,), device_id_type=MESH)

    @pl.when(has_high)
    def _():
        pl.semaphore_signal(barrier, inc=1, device_id=(upper,), device_id_type=MESH)

    pl.semaphore_wait(barrier, len(partners) + jnp.where(has_low, 1, 0) + jnp.where(has_high, 1, 0))

    def rows_of(b):
        return slice(b * block, (b + 1) * block)

    class Halo:
        def __init__(self, slot, to_upper, from_lower, to_lower, from_upper):
            def copy(way, i, source, target, device):
                return pltpu.make_async_remote_copy(
                    src_ref=source.at[pl.ds(i * block, block)], dst_ref=target.at[pl.ds(i * block, block)],
                    send_sem=halo_send.at[slot, way, i], recv_sem=halo_recv.at[slot, way, i],
                    device_id=(device,), device_id_type=MESH)

            self.ups = [copy(0, i, to_upper, from_lower, upper) for i in range(here)]
            self.downs = [copy(1, i, to_lower, from_upper, lower) for i in range(here)]
            self.from_lower, self.from_upper = from_lower, from_upper

        def clear(self):
            @pl.when(jnp.logical_not(has_low))
            def _():
                self.from_lower[...] = jnp.zeros(self.from_lower.shape, F32)

            @pl.when(jnp.logical_not(has_high))
            def _():
                self.from_upper[...] = jnp.zeros(self.from_upper.shape, F32)

        def up(self, i):
            @pl.when(has_high)
            def _():
                self.ups[i].start()

        def down(self, i):
            @pl.when(has_low)
            def _():
                self.downs[i].start()

        def wait_lower(self, i):
            @pl.when(has_low)
            def _():
                self.ups[i].wait_recv()

        def wait_upper(self, i):
            @pl.when(has_high)
            def _():
                self.downs[i].wait_recv()

        def sent(self):
            @pl.when(has_high)
            def _():
                for copy in self.ups:
                    copy.wait_send()

            @pl.when(has_low)
            def _():
                for copy in self.downs:
                    copy.wait_send()

    first = Halo(0, features, far_features.at[0], features, far_features.at[1])
    for i in range(here):
        first.up(here - 1 - i)
        first.down(i)
    first.clear()

    win_high[...], win_low[...] = split(weight_in[...])
    wout_high[...], wout_low[...] = split(weight_out[...])
    back_high[...], back_low[...] = split(weight_out[...].T)
    middle = slice(own, 2 * own)
    near_high[middle, :], near_low[middle, :] = split(features[...])
    for b in range(here):
        lanes = lax.broadcasted_iota(jnp.int32, (classes, block), 0)
        onehot_ref[rows_of(b), :] = jnp.where(labels[:, rows_of(b)] == lanes, 1.0, 0.0).astype(F32).T
    fetch.wait()
    for b in range(here):
        weights = []
        for k in range(slots):
            relative = index_ref[b, k] - (me * here - REACH) - b
            used = k < counts_ref[b]
            weights.append([
                jnp.where(jnp.logical_and(used, relative == j), 1.0, 0.0).astype(F32) for j in range(wide)])

        def densify(rows, b=b, weights=weights):
            sums = [None] * wide
            for k in range(slots):
                tile = adjacency[b, k, rows, :]
                for j in range(wide):
                    term = weights[k][j] * tile
                    sums[j] = term if k == 0 else sums[j] + term
            for j in range(wide):
                columns = rows_of(j)
                high, low = split(sums[j])
                band[b, rows, columns] = sums[j]
                band_high[b, rows, columns] = high
                band_low[b, rows, columns] = low

        chunks(block, 32, densify)

    def propagate(total, high, low, b, first_block, last_block, fresh=False):
        first_block, last_block = max(first_block, b), min(last_block, b + wide - 1)
        if first_block > last_block:
            return
        columns = slice((first_block - b) * block, (last_block - b + 1) * block)
        window = slice(first_block * block, (last_block + 1) * block)
        value = mm(band_high[b, :, columns], band_low[b, :, columns], high[window, :], low[window, :])
        total[rows_of(b), :] = value if fresh else total[rows_of(b), :] + value

    for b in range(here):
        propagate(spread, near_high, near_low, b, REACH, REACH + here - 1, fresh=True)
    for b in range(here):
        for j in range(wide):
            high, low = split(band[b, :, rows_of(j)].T)
            turned_high[b, rows_of(j), :] = high
            turned_low[b, rows_of(j), :] = low

    def arrive_features(side, i):
        if side == 0:
            first.wait_lower(i)
        else:
            first.wait_upper(i)
        place = i if side == 0 else REACH + here + i
        near_high[rows_of(place), :], near_low[rows_of(place), :] = split(far_features[side, rows_of(i), :])
        for b in range(here):
            propagate(spread, near_high, near_low, b, place, place)

    second = Halo(
        1, near_z.at[pl.ds(own, own)], near_z.at[pl.ds(0, own)],
        near_z.at[pl.ds(own, own)], near_z.at[pl.ds(2 * own, own)])

    def forward(b):
        rows = rows_of(b)
        spread_high[rows, :], spread_low[rows, :] = split(spread[rows, :])
        slope[rows, :] = mm(spread_high[rows, :], spread_low[rows, :], win_high[...], win_low[...])

        def gelu(i, carry):
            part = pl.ds(pl.multiple_of(b * block + i * 32, 32), 32)
            x = slope[part, :]
            below = 0.5 * (1.0 + lax.erf(x * 0.7071067811865476))
            value = x * below
            hidden[part, :] = value
            hid_high[part, :], hid_low[part, :] = split(value)
            slope[part, :] = below + x * (jnp.exp(-0.5 * x * x) * 0.3989422804014327)
            return carry

        lax.fori_loop(0, block // 32, gelu, 0)
        near_z[own + b * block : own + (b + 1) * block, :] = mm(
            hid_high[rows, :], hid_low[rows, :], wout_high[...], wout_low[...])
        second.up(b)
        second.down(b)

    arrive_features(0, 1)
    arrive_features(1, 0)
    arrive_features(0, 0)
    forward(0)
    arrive_features(1, 1)
    forward(1)
    second.clear()

    z_high[middle, :], z_low[middle, :] = split(near_z[middle, :])
    for b in range(here):
        propagate(logits_ref, z_high, z_low, b, REACH, REACH + here - 1, fresh=True)
    for b in range(here):
        rows = rows_of(b)
        spread_t_high[:, rows], spread_t_low[:, rows] = split(spread[rows, :].T)
        for c in range(hid // block):
            hid_t_high[rows_of(c), rows], hid_t_low[rows_of(c), rows] = split(hidden[rows, rows_of(c)].T)
    for i in range(here):
        second.wait_lower(i)
        second.wait_upper(i)
        for place in (i, REACH + here + i):
            z_high[rows_of(place), :], z_low[rows_of(place), :] = split(near_z[rows_of(place), :])
            for b in range(here):
                propagate(logits_ref, z_high, z_low, b, place, place)
    place_logits = pltpu.make_async_copy(logits_ref, logits_out, local_sem.at[0])
    place_logits.start()

    loss_acc[...] = jnp.zeros(loss_acc.shape, F32)
    third = Halo(2, out_high, in_low, out_low, in_high)

    def softmax(b):
        rows = rows_of(b)
        logits = logits_ref[rows, :]
        totals = jnp.log(jnp.sum(jnp.exp(logits), axis=1, keepdims=True))
        onehot = onehot_ref[rows, :]
        row_loss = totals - jnp.sum(onehot * logits, axis=1, keepdims=True)
        loss_acc[...] += jnp.broadcast_to(jnp.sum(row_loss, axis=0, keepdims=True), loss_acc.shape)
        grad_high[rows, :], grad_low[rows, :] = split(jnp.exp(logits - totals) - onehot)

    def bucket(place):
        total = None
        for b in range(here):
            if 0 <= place - b < wide:
                term = mm(
                    turned_high[b, rows_of(place - b), :], turned_low[b, rows_of(place - b), :],
                    grad_high[rows_of(b), :], grad_low[rows_of(b), :])
                total = term if total is None else total + term
        return total

    softmax(0)
    out_low[rows_of(0), :] = bucket(0)
    third.down(0)
    softmax(1)
    for i in range(here):
        out_high[rows_of(i), :] = bucket(REACH + here + i)
        third.up(i)
        if i > 0:
            out_low[rows_of(i), :] = bucket(i)
            third.down(i)
    third.clear()
    for i in range(here):
        returned[rows_of(i), :] = bucket(REACH + i)

    lows = [0] * PARTS
    stages = [
        [(0, s) for s in range(len(part))] + [(1, s) for s in reversed(range(len(part))) if part[s][4]] for part in steps]
    reached = [0] * PARTS
    flying = [None] * PARTS

    def start_stage(part):
        phase, s = stages[part][reached[part]]
        group, length, offset, message, cuts = steps[part][s]
        low, copies = lows[part], []
        if phase == 1 and (reached[part] == 0 or stages[part][reached[part] - 1][0] == 0):
            rows = pl.ds(pl.multiple_of(low, SMALLEST), length)
            full[part, rows, :] = acc[part, rows, :]
        for delta in range(1, 1 << len(group)):
            other, theirs, mine = member(group, delta)
            if phase == 0:
                start = low + theirs * length if cuts else low
                source = acc.at[part, pl.ds(pl.multiple_of(start, SMALLEST), length)]
                target = landing.at[part, pl.ds(offset + (delta - 1) * length, length)]
            else:
                source = target = full.at[part, pl.ds(pl.multiple_of(low, SMALLEST), length)]
            copy = pltpu.make_async_remote_copy(
                src_ref=source, dst_ref=target, send_sem=part_send.at[phase, part, message + delta - 1],
                recv_sem=part_recv.at[phase, part, message + delta - 1], device_id=(other,), device_id_type=MESH)
            copy.start()
            copies.append(copy)
        if cuts:
            lows[part] = low + mine * length if phase == 0 else low - mine * length
        flying[part] = copies

    def finish_stage(part):
        phase, s = stages[part][reached[part]]
        group, length, offset, _, _ = steps[part][s]
        for copy in flying[part]:
            copy.wait()
        if phase == 0:
            rows = pl.ds(pl.multiple_of(lows[part], SMALLEST), length)
            total = acc[part, rows, :]
            for i in range(len(flying[part])):
                total = total + landing[part, pl.ds(offset + i * length, length), :]
            acc[part, rows, :] = total
        reached[part] += 1

    loss_flying = []

    def start_loss(s):
        group, _, _, message, _ = steps[0][s]
        loss_flying.clear()
        for delta in range(1, 1 << len(group)):
            other, _, _ = member(group, delta)
            place = message + delta - 1
            copy = pltpu.make_async_remote_copy(
                src_ref=loss_acc, dst_ref=loss_in.at[place], send_sem=loss_send.at[place], recv_sem=loss_recv.at[place],
                device_id=(other,), device_id_type=MESH)
            copy.start()
            loss_flying.append(copy)

    def finish_loss(s):
        for copy in loss_flying:
            copy.wait()
        total = loss_acc[...]
        for i in range(len(loss_flying)):
            total = total + loss_in[steps[0][s][3] + i]
        loss_acc[...] = total

    start_loss(0)
    values = [None] * 2
    for b in range(here):
        rows = rows_of(b)
        third.wait_lower(b)
        third.wait_upper(b)
        ret_high[rows, :], ret_low[rows, :] = split(returned[rows, :] + (in_low[rows, :] + in_high[rows, :]))
        value = mm(hid_t_high[:, rows], hid_t_low[:, rows], ret_high[rows, :], ret_low[rows, :])
        acc[2] = value if b == 0 else acc[2] + value
        if b == here - 1:
            start_stage(2)
        hidden_grad[rows, :] = mm(ret_high[rows, :], ret_low[rows, :], back_high[...], back_low[...])

        def pre_grad(i, carry, b=b):
            part = pl.ds(pl.multiple_of(b * block + i * 32, 32), 32)
            hid_high[part, :], hid_low[part, :] = split(hidden_grad[part, :] * slope[part, :])
            return carry

        lax.fori_loop(0, block // 32, pre_grad, 0)
        if b == here - 1:
            place_hidden = pltpu.make_async_copy(hidden_grad, hidden_grad_out, local_sem.at[1])
            place_hidden.start()
            finish_stage(2)
            start_stage(2)
            finish_loss(0)
            start_loss(1)
        for part in range(2):
            columns = slice(part * hid // 2, (part + 1) * hid // 2)
            value = mm(spread_t_high[:, rows], spread_t_low[:, rows], hid_high[rows, columns], hid_low[rows, columns])
            for i in range(2):
                piece = value[:, i * classes : (i + 1) * classes]
                acc[part, rows_of(i), :] = piece if b == 0 else acc[part, rows_of(i), :] + piece
            if b == here - 1:
                start_stage(part)

    placing = []
    loss_step = 1
    while any(reached[part] < len(stages[part]) for part in range(PARTS)):
        for part in (2, 0, 1):
            if reached[part] == len(stages[part]):
                continue
            finish_stage(part)
            if reached[part] < len(stages[part]):
                start_stage(part)
            else:
                copy = pltpu.make_async_copy(full.at[part], packed_out.at[part], local_sem.at[2 + part])
                copy.start()
                placing.append(copy)
        if loss_step < len(steps[0]):
            finish_loss(loss_step)
            loss_step += 1
            if loss_step < len(steps[0]):
                start_loss(loss_step)
            else:
                loss_out[...] = loss_acc[...]
    for halo in (first, second, third):
        halo.sent()
    for copy in [place_logits, place_hidden] + placing:
        copy.wait()


def place(total, logits, loss, hidden_grad, packed, logits_out, loss_out, hidden_grad_out, grad_in_out, grad_out_out, sems):
    f_in, hid = grad_in_out.shape
    classes = logits.shape[1]
    loss_out[0, 0] = loss[0, 0] * (1.0 / total)
    quarter = hidden_grad.shape[0] // 4
    pairs = [(logits, logits_out), (packed.at[2], grad_out_out)]
    for i in range(4):
        rows = pl.ds(i * quarter, quarter)
        pairs.append((hidden_grad.at[rows], hidden_grad_out.at[rows]))
    for i in range(hid // classes):
        pairs.append((
            packed.at[i // 2, pl.ds(i % 2 * f_in, f_in)], grad_in_out.at[:, pl.ds(i * classes, classes)]))
    copies = [pltpu.make_async_copy(source, target, sems.at[i]) for i, (source, target) in enumerate(pairs)]
    for copy in copies:
        copy.start()
    for copy in copies:
        copy.wait()


def per_device(n, features, adjacency, block_index, block_counts, labels, weight_in, weight_out):
    own, f_in = features.shape
    here, _, block, _ = adjacency.shape
    hid, classes = weight_out.shape
    wide = 2 * REACH + 1
    rows = hid
    steps, landing, messages = plan(n, rows)

    def both(*shape):
        return [pltpu.VMEM(shape, BF16)] * 2

    def plain(*shape):
        return pltpu.VMEM(shape, F32)

    scratch = [
        plain(*adjacency.shape), plain(2, own, f_in), plain(here, block, wide * block), *both(here, block, wide * block),
        *both(here, wide * block, block), *both(3 * own, f_in), *both(f_in, hid), *both(hid, classes),
        *both(classes, hid), *both(own, f_in), *both(f_in, own), plain(own, f_in), plain(own, hid), plain(own, hid),
        *both(own, hid), *both(hid, own), plain(own, classes), plain(3 * own, classes), *both(3 * own, classes),
        plain(own, classes), *both(own, classes),
        plain(own, classes), plain(own, classes), plain(own, classes), plain(own, classes), plain(own, classes),
        *both(own, classes), plain(own, hid),
        plain(PARTS, rows, classes), plain(PARTS, landing, classes), plain(PARTS, rows, classes),
        plain(8, 128), plain(messages, 8, 128),
        pltpu.SemaphoreType.DMA((3, 2, here)), pltpu.SemaphoreType.DMA((3, 2, here)),
        pltpu.SemaphoreType.DMA((2, PARTS, messages)), pltpu.SemaphoreType.DMA((2, PARTS, messages)),
        pltpu.SemaphoreType.DMA((messages,)), pltpu.SemaphoreType.DMA((messages,)),
        pltpu.SemaphoreType.DMA((2 + PARTS,)),
    ]
    smem, vmem, hbm = (pl.BlockSpec(memory_space=space) for space in (pltpu.SMEM, pltpu.VMEM, pltpu.HBM))

    def arrays(*shapes):
        return [jax.ShapeDtypeStruct(shape, F32) for shape in shapes]

    logits, loss, hidden_grad, packed = pl.pallas_call(
        functools.partial(kernel, n, steps),
        out_shape=arrays((own, classes), (8, 128), (own, hid), (PARTS, rows, classes)),
        in_specs=[smem, smem, vmem, hbm, vmem, vmem, vmem],
        out_specs=[hbm, vmem, hbm, hbm],
        scratch_shapes=scratch,
        compiler_params=pltpu.CompilerParams(
            collective_id=0, has_side_effects=True, vmem_limit_bytes=56 * 1024 * 1024),
        name="step",
    )(block_index, block_counts, features, adjacency, labels[None, :], weight_in, weight_out)
    logits, loss, hidden_grad, grad_in, grad_out = pl.pallas_call(
        functools.partial(place, float(own * n)),
        out_shape=arrays((own, classes), (1, 1), (own, hid), (f_in, hid), (hid, classes)),
        in_specs=[hbm, smem, hbm, hbm],
        out_specs=[hbm, smem, hbm, hbm, hbm],
        scratch_shapes=[pltpu.SemaphoreType.DMA((6 + hid // classes,))],
        compiler_params=pltpu.CompilerParams(vmem_limit_bytes=63 * 1024 * 1024),
        name="place",
    )(logits, loss, hidden_grad, packed)
    return (logits, loss[0, 0], hidden_grad, grad_in, grad_out)


def solution(mesh):
    in_specs = (
        P("rows", None),
        P("rows", None, None, None),
        P("rows", None),
        P("rows"),
        P("rows"),
        P(),
        P(),
    )
    out_specs = (P("rows", None), P(), P("rows", None), P(), P())
    return jax.shard_map(
        functools.partial(per_device, mesh.shape["rows"]),
        mesh=mesh, in_specs=in_specs, out_specs=out_specs, check_vma=False,
    )
```

```python
import functools

import jax
import jax.numpy as jnp
from jax import lax
from jax.experimental import pallas as pl
from jax.experimental.pallas import tpu as pltpu
from jax.sharding import PartitionSpec as P

REACH = 2
F32 = jnp.float32
BF16 = jnp.bfloat16
MESH = pl.DeviceIdType.MESH
PARTS = 3
SMALLEST = 16
TOGETHER = 3


def split(value):
    high = value.astype(BF16)
    return high, (value - high.astype(F32)).astype(BF16)


def mm(a_high, a_low, b_high, b_low):
    def one(a, b):
        return jnp.dot(a, b, preferred_element_type=F32)

    return one(a_high, b_high) + (one(a_high, b_low) + one(a_low, b_high))


def mm_beside(a_high, a_low, b_both):
    width = b_both.shape[1] // 2
    wide = jnp.dot(a_high, b_both, preferred_element_type=F32)
    return wide[:, :width] + (wide[:, width:] + jnp.dot(a_low, b_both[:, :width], preferred_element_type=F32))


def chunks(total, size, body):
    def step(i, carry):
        body(pl.ds(pl.multiple_of(i * size, size), size))
        return carry

    lax.fori_loop(0, total // size, step, 0)


def plan(n, rows):
    bits = list(range(n.bit_length() - 1))
    cut = min(len(bits), (rows // SMALLEST).bit_length() - 1)
    parts = []
    for part in range(PARTS):
        near = bits[1:4]
        turn = part % max(1, len(near))
        order = bits[:1] + near[turn:] + near[:turn] + bits[4:]
        groups = [(bit,) for bit in order[: cut - TOGETHER]] + [tuple(order[cut - TOGETHER : cut])] + [(bit,) for bit in order[cut:]]
        length, offset, message, steps = rows, 0, 0, []
        for number, group in enumerate(groups):
            members = 1 << len(group)
            cuts = number < cut - TOGETHER + 1
            if cuts:
                length //= members
            steps.append((group, length, offset, message, cuts))
            offset += (members - 1) * length
            message += members - 1
        parts.append(steps)
    return parts, offset, message


def kernel(
    n, steps, index_ref, counts_ref, features, adjacency_hbm, labels, weight_in, weight_out,
    logits_out, loss_out, hidden_grad_out, packed_out,
    adjacency, far_features, band, band_high, band_low, turned_high, turned_low,
    near_high, near_low, win_high, win_low, wout_both, back_high, back_low,
    spread_high, spread_low, spread_t_high, spread_t_low, spread, hidden, slope, hid_high, hid_low, hid_t_high, hid_t_low,
    onehot_ref, near_z, z_both, logits_ref, grad_both, out_low, out_high, in_low, in_high, returned,
    ret_both, hidden_grad, acc, landing, full, loss_acc, loss_in,
    halo_send, halo_recv, part_send, part_recv, loss_send, loss_recv, local_sem,
):
    me = lax.axis_index("rows")
    own = features.shape[0]
    here, slots, block = adjacency.shape[:3]
    wide = 2 * REACH + 1
    hid = weight_in.shape[1]
    classes = weight_out.shape[1]
    has_low, has_high = me > 0, me < n - 1
    lower, upper = jnp.maximum(me - 1, 0), jnp.minimum(me + 1, n - 1)

    fetch = pltpu.make_async_copy(adjacency_hbm, adjacency, local_sem.at[0])
    fetch.start()

    def bit_of(bit):
        return lax.rem(lax.div(me, 1 << bit), 2)

    def member(group, delta):
        other, theirs, mine = me, 0, 0
        for position, bit in enumerate(group):
            weight = 1 << (len(group) - 1 - position)
            value = bit_of(bit)
            mine = mine + value * weight
            if delta & weight:
                other = other + (1 - 2 * value) * (1 << bit)
                theirs = theirs + (1 - value) * weight
            else:
                theirs = theirs + value * weight
        return other, theirs, mine

    partners = sorted({
        sum(1 << bit for position, bit in enumerate(step[0]) if delta & (1 << (len(step[0]) - 1 - position)))
        for part in steps for step in part for delta in range(1, 1 << len(step[0]))})
    barrier = pltpu.get_barrier_semaphore()
    for mask in partners:
        other = me
        for bit in range(n.bit_length() - 1):
            if mask >> bit & 1:
                other = other + (1 - 2 * bit_of(bit)) * (1 << bit)
        pl.semaphore_signal(barrier, inc=1, device_id=(other,), device_id_type=MESH)

    @pl.when(has_low)
    def _():
        pl.semaphore_signal(barrier, inc=1, device_id=(lower,), device_id_type=MESH)

    @pl.when(has_high)
    def _():
        pl.semaphore_signal(barrier, inc=1, device_id=(upper,), device_id_type=MESH)

    pl.semaphore_wait(barrier, len(partners) + jnp.where(has_low, 1, 0) + jnp.where(has_high, 1, 0))

    def rows_of(b):
        return slice(b * block, (b + 1) * block)

    class Halo:
        def __init__(self, slot, to_upper, from_lower, to_lower, from_upper):
            def copy(way, i, source, target, device):
                return pltpu.make_async_remote_copy(
                    src_ref=source.at[pl.ds(i * block, block)], dst_ref=target.at[pl.ds(i * block, block)],
                    send_sem=halo_send.at[slot, way, i], recv_sem=halo_recv.at[slot, way, i],
                    device_id=(device,), device_id_type=MESH)

            self.ups = [copy(0, i, to_upper, from_lower, upper) for i in range(here)]
            self.downs = [copy(1, i, to_lower, from_upper, lower) for i in range(here)]
            self.from_lower, self.from_upper = from_lower, from_upper

        def clear(self):
            @pl.when(jnp.logical_not(has_low))
            def _():
                self.from_lower[...] = jnp.zeros(self.from_lower.shape, F32)

            @pl.when(jnp.logical_not(has_high))
            def _():
                self.from_upper[...] = jnp.zeros(self.from_upper.shape, F32)

        def up(self, i):
            @pl.when(has_high)
            def _():
                self.ups[i].start()

        def down(self, i):
            @pl.when(has_low)
            def _():
                self.downs[i].start()

        def wait_lower(self, i):
            @pl.when(has_low)
            def _():
                self.ups[i].wait_recv()

        def wait_upper(self, i):
            @pl.when(has_high)
            def _():
                self.downs[i].wait_recv()

        def sent(self):
            @pl.when(has_high)
            def _():
                for copy in self.ups:
                    copy.wait_send()

            @pl.when(has_low)
            def _():
                for copy in self.downs:
                    copy.wait_send()

    first = Halo(0, features, far_features.at[0], features, far_features.at[1])
    for i in range(here):
        first.up(here - 1 - i)
        first.down(i)
    first.clear()

    win_high[...], win_low[...] = split(weight_in[...])
    wout_both[:, :classes], wout_both[:, classes:] = split(weight_out[...])
    back_high[...], back_low[...] = split(weight_out[...].T)
    middle = slice(own, 2 * own)
    near_high[middle, :], near_low[middle, :] = split(features[...])
    for b in range(here):
        lanes = lax.broadcasted_iota(jnp.int32, (classes, block), 0)
        onehot_ref[rows_of(b), :] = jnp.where(labels[:, rows_of(b)] == lanes, 1.0, 0.0).astype(F32).T
    fetch.wait()
    for b in range(here):
        weights = []
        for k in range(slots):
            relative = index_ref[b, k] - (me * here - REACH) - b
            used = k < counts_ref[b]
            weights.append([
                jnp.where(jnp.logical_and(used, relative == j), 1.0, 0.0).astype(F32) for j in range(wide)])

        def densify(rows, b=b, weights=weights):
            sums = [None] * wide
            for k in range(slots):
                tile = adjacency[b, k, rows, :]
                for j in range(wide):
                    term = weights[k][j] * tile
                    sums[j] = term if k == 0 else sums[j] + term
            for j in range(wide):
                columns = rows_of(j)
                high, low = split(sums[j])
                band[b, rows, columns] = sums[j]
                band_high[b, rows, columns] = high
                band_low[b, rows, columns] = low

        chunks(block, 32, densify)

    def propagate(total, high, low, b, first_block, last_block, fresh=False):
        first_block, last_block = max(first_block, b), min(last_block, b + wide - 1)
        if first_block > last_block:
            return
        columns = slice((first_block - b) * block, (last_block - b + 1) * block)
        window = slice(first_block * block, (last_block + 1) * block)
        if low is None:
            value = mm_beside(band_high[b, :, columns], band_low[b, :, columns], high[window, :])
        else:
            value = mm(band_high[b, :, columns], band_low[b, :, columns], high[window, :], low[window, :])
        total[rows_of(b), :] = value if fresh else total[rows_of(b), :] + value

    for b in range(here):
        propagate(spread, near_high, near_low, b, REACH, REACH + here - 1, fresh=True)
    for b in range(here):
        for j in range(wide):
            high, low = split(band[b, :, rows_of(j)].T)
            turned_high[b, rows_of(j), :] = high
            turned_low[b, rows_of(j), :] = low

    def arrive_features(side, i):
        if side == 0:
            first.wait_lower(i)
        else:
            first.wait_upper(i)
        place = i if side == 0 else REACH + here + i
        near_high[rows_of(place), :], near_low[rows_of(place), :] = split(far_features[side, rows_of(i), :])
        for b in range(here):
            propagate(spread, near_high, near_low, b, place, place)

    second = Halo(
        1, near_z.at[pl.ds(own, own)], near_z.at[pl.ds(0, own)],
        near_z.at[pl.ds(own, own)], near_z.at[pl.ds(2 * own, own)])

    def forward(b):
        rows = rows_of(b)
        spread_high[rows, :], spread_low[rows, :] = split(spread[rows, :])
        slope[rows, :] = mm(spread_high[rows, :], spread_low[rows, :], win_high[...], win_low[...])

        def gelu(i, carry):
            part = pl.ds(pl.multiple_of(b * block + i * 32, 32), 32)
            x = slope[part, :]
            below = 0.5 * (1.0 + lax.erf(x * 0.7071067811865476))
            value = x * below
            hidden[part, :] = value
            hid_high[part, :], hid_low[part, :] = split(value)
            slope[part, :] = below + x * (jnp.exp(-0.5 * x * x) * 0.3989422804014327)
            return carry

        lax.fori_loop(0, block // 32, gelu, 0)
        near_z[own + b * block : own + (b + 1) * block, :] = mm_beside(
            hid_high[rows, :], hid_low[rows, :], wout_both[...])
        second.up(b)
        second.down(b)

    arrive_features(0, 1)
    arrive_features(1, 0)
    arrive_features(0, 0)
    forward(0)
    arrive_features(1, 1)
    forward(1)
    second.clear()

    z_both[middle, :classes], z_both[middle, classes:] = split(near_z[middle, :])
    for b in range(here):
        propagate(logits_ref, z_both, None, b, REACH, REACH + here - 1, fresh=True)
    for b in range(here):
        rows = rows_of(b)
        spread_t_high[:, rows], spread_t_low[:, rows] = split(spread[rows, :].T)
        for c in range(hid // block):
            hid_t_high[rows_of(c), rows], hid_t_low[rows_of(c), rows] = split(hidden[rows, rows_of(c)].T)
    for i in range(here):
        second.wait_lower(i)
        second.wait_upper(i)
        for place in (i, REACH + here + i):
            z_both[rows_of(place), :classes], z_both[rows_of(place), classes:] = split(near_z[rows_of(place), :])
            for b in range(here):
                propagate(logits_ref, z_both, None, b, place, place)
    place_logits = pltpu.make_async_copy(logits_ref, logits_out, local_sem.at[0])
    place_logits.start()

    loss_acc[...] = jnp.zeros(loss_acc.shape, F32)
    third = Halo(2, out_high, in_low, out_low, in_high)

    def softmax(b):
        rows = rows_of(b)
        logits = logits_ref[rows, :]
        totals = jnp.log(jnp.sum(jnp.exp(logits), axis=1, keepdims=True))
        onehot = onehot_ref[rows, :]
        row_loss = totals - jnp.sum(onehot * logits, axis=1, keepdims=True)
        loss_acc[...] += jnp.broadcast_to(jnp.sum(row_loss, axis=0, keepdims=True), loss_acc.shape)
        grad_both[rows, :classes], grad_both[rows, classes:] = split(jnp.exp(logits - totals) - onehot)

    def bucket(place):
        total = None
        for b in range(here):
            if 0 <= place - b < wide:
                term = mm_beside(
                    turned_high[b, rows_of(place - b), :], turned_low[b, rows_of(place - b), :],
                    grad_both[rows_of(b), :])
                total = term if total is None else total + term
        return total

    softmax(0)
    out_low[rows_of(0), :] = bucket(0)
    third.down(0)
    softmax(1)
    for i in range(here):
        out_high[rows_of(i), :] = bucket(REACH + here + i)
        third.up(i)
        if i > 0:
            out_low[rows_of(i), :] = bucket(i)
            third.down(i)
    third.clear()
    for i in range(here):
        returned[rows_of(i), :] = bucket(REACH + i)

    lows = [0] * PARTS
    stages = [
        [(0, s) for s in range(len(part))] + [(1, s) for s in reversed(range(len(part))) if part[s][4]] for part in steps]
    reached = [0] * PARTS
    flying = [None] * PARTS

    def start_stage(part):
        phase, s = stages[part][reached[part]]
        group, length, offset, message, cuts = steps[part][s]
        low, copies = lows[part], []
        if phase == 1 and (reached[part] == 0 or stages[part][reached[part] - 1][0] == 0):
            rows = pl.ds(pl.multiple_of(low, SMALLEST), length)
            full[part, rows, :] = acc[part, rows, :]
        for delta in range(1, 1 << len(group)):
            other, theirs, mine = member(group, delta)
            if phase == 0:
                start = low + theirs * length if cuts else low
                source = acc.at[part, pl.ds(pl.multiple_of(start, SMALLEST), length)]
                target = landing.at[part, pl.ds(offset + (delta - 1) * length, length)]
            else:
                source = target = full.at[part, pl.ds(pl.multiple_of(low, SMALLEST), length)]
            copy = pltpu.make_async_remote_copy(
                src_ref=source, dst_ref=target, send_sem=part_send.at[phase, part, message + delta - 1],
                recv_sem=part_recv.at[phase, part, message + delta - 1], device_id=(other,), device_id_type=MESH)
            copy.start()
            copies.append(copy)
        if cuts:
            lows[part] = low + mine * length if phase == 0 else low - mine * length
        flying[part] = copies

    def finish_stage(part):
        phase, s = stages[part][reached[part]]
        group, length, offset, _, _ = steps[part][s]
        for copy in flying[part]:
            copy.wait()
        if phase == 0:
            rows = pl.ds(pl.multiple_of(lows[part], SMALLEST), length)
            total = acc[part, rows, :]
            for i in range(len(flying[part])):
                total = total + landing[part, pl.ds(offset + i * length, length), :]
            acc[part, rows, :] = total
        reached[part] += 1

    loss_flying = []

    def start_loss(s):
        group, _, _, message, _ = steps[0][s]
        loss_flying.clear()
        for delta in range(1, 1 << len(group)):
            other, _, _ = member(group, delta)
            place = message + delta - 1
            copy = pltpu.make_async_remote_copy(
                src_ref=loss_acc, dst_ref=loss_in.at[place], send_sem=loss_send.at[place], recv_sem=loss_recv.at[place],
                device_id=(other,), device_id_type=MESH)
            copy.start()
            loss_flying.append(copy)

    def finish_loss(s):
        for copy in loss_flying:
            copy.wait()
        total = loss_acc[...]
        for i in range(len(loss_flying)):
            total = total + loss_in[steps[0][s][3] + i]
        loss_acc[...] = total

    start_loss(0)
    values = [None] * 2
    for b in range(here):
        rows = rows_of(b)
        third.wait_lower(b)
        third.wait_upper(b)
        ret_both[rows, :classes], ret_both[rows, classes:] = split(returned[rows, :] + (in_low[rows, :] + in_high[rows, :]))
        value = mm_beside(hid_t_high[:, rows], hid_t_low[:, rows], ret_both[rows, :])
        acc[2] = value if b == 0 else acc[2] + value
        if b == here - 1:
            start_stage(2)
        hidden_grad[rows, :] = mm(ret_both[rows, :classes], ret_both[rows, classes:], back_high[...], back_low[...])

        def pre_grad(i, carry, b=b):
            part = pl.ds(pl.multiple_of(b * block + i * 32, 32), 32)
            hid_high[part, :], hid_low[part, :] = split(hidden_grad[part, :] * slope[part, :])
            return carry

        lax.fori_loop(0, block // 32, pre_grad, 0)
        if b == here - 1:
            place_hidden = pltpu.make_async_copy(hidden_grad, hidden_grad_out, local_sem.at[1])
            place_hidden.start()
            finish_stage(2)
            start_stage(2)
            finish_loss(0)
            start_loss(1)
        for part in range(2):
            columns = slice(part * hid // 2, (part + 1) * hid // 2)
            value = mm(spread_t_high[:, rows], spread_t_low[:, rows], hid_high[rows, columns], hid_low[rows, columns])
            for i in range(2):
                piece = value[:, i * classes : (i + 1) * classes]
                acc[part, rows_of(i), :] = piece if b == 0 else acc[part, rows_of(i), :] + piece
            if b == here - 1:
                start_stage(part)

    placing = []
    loss_step = 1
    while any(reached[part] < len(stages[part]) for part in range(PARTS)):
        for part in (2, 0, 1):
            if reached[part] == len(stages[part]):
                continue
            finish_stage(part)
            if reached[part] < len(stages[part]):
                start_stage(part)
            else:
                copy = pltpu.make_async_copy(full.at[part], packed_out.at[part], local_sem.at[2 + part])
                copy.start()
                placing.append(copy)
        if loss_step < len(steps[0]):
            finish_loss(loss_step)
            loss_step += 1
            if loss_step < len(steps[0]):
                start_loss(loss_step)
            else:
                loss_out[...] = loss_acc[...]
    for halo in (first, second, third):
        halo.sent()
    for copy in [place_logits, place_hidden] + placing:
        copy.wait()


def place(
    total, logits, loss, hidden_grad, packed, logits_out, loss_out, hidden_grad_out, grad_in_out, grad_out_out,
    logits_here, hidden_here, packed_here, sems,
):
    f_in, hid = grad_in_out.shape
    classes = logits.shape[1]
    quarter = hidden_grad.shape[0] // 4
    moves = []
    for i in range(4):
        rows = pl.ds(i * quarter, quarter)
        moves.append((hidden_grad.at[rows], hidden_here.at[rows], hidden_grad_out.at[rows]))
    for i in range(hid // classes):
        piece = (i // 2, pl.ds(i % 2 * f_in, f_in))
        moves.append((packed.at[piece], packed_here.at[piece], grad_in_out.at[:, pl.ds(i * classes, classes)]))
    moves.append((packed.at[2], packed_here.at[2], grad_out_out))
    moves.append((logits, logits_here, logits_out))
    fetches = [pltpu.make_async_copy(source, via, sems.at[0, i]) for i, (source, via, _) in enumerate(moves)]
    stores = [pltpu.make_async_copy(via, target, sems.at[1, i]) for i, (_, via, target) in enumerate(moves)]
    for copy in fetches:
        copy.start()
    loss_out[0, 0] = loss[0, 0] * (1.0 / total)
    for fetch, store in zip(fetches, stores):
        fetch.wait()
        store.start()
    for copy in stores:
        copy.wait()


def per_device(n, features, adjacency, block_index, block_counts, labels, weight_in, weight_out):
    own, f_in = features.shape
    here, _, block, _ = adjacency.shape
    hid, classes = weight_out.shape
    wide = 2 * REACH + 1
    rows = hid
    steps, landing, messages = plan(n, rows)

    def both(*shape):
        return [pltpu.VMEM(shape, BF16)] * 2

    def beside(length):
        return pltpu.VMEM((length, 2 * classes), BF16)

    def plain(*shape):
        return pltpu.VMEM(shape, F32)

    scratch = [
        plain(*adjacency.shape), plain(2, own, f_in), plain(here, block, wide * block), *both(here, block, wide * block),
        *both(here, wide * block, block), *both(3 * own, f_in), *both(f_in, hid), beside(hid),
        *both(classes, hid), *both(own, f_in), *both(f_in, own), plain(own, f_in), plain(own, hid), plain(own, hid),
        *both(own, hid), *both(hid, own), plain(own, classes), plain(3 * own, classes), beside(3 * own),
        plain(own, classes), beside(own),
        plain(own, classes), plain(own, classes), plain(own, classes), plain(own, classes), plain(own, classes),
        beside(own), plain(own, hid),
        plain(PARTS, rows, classes), plain(PARTS, landing, classes), plain(PARTS, rows, classes),
        plain(8, 128), plain(messages, 8, 128),
        pltpu.SemaphoreType.DMA((3, 2, here)), pltpu.SemaphoreType.DMA((3, 2, here)),
        pltpu.SemaphoreType.DMA((2, PARTS, messages)), pltpu.SemaphoreType.DMA((2, PARTS, messages)),
        pltpu.SemaphoreType.DMA((messages,)), pltpu.SemaphoreType.DMA((messages,)),
        pltpu.SemaphoreType.DMA((2 + PARTS,)),
    ]
    smem, vmem, hbm = (pl.BlockSpec(memory_space=space) for space in (pltpu.SMEM, pltpu.VMEM, pltpu.HBM))

    def arrays(*shapes):
        return [jax.ShapeDtypeStruct(shape, F32) for shape in shapes]

    logits, loss, hidden_grad, packed = pl.pallas_call(
        functools.partial(kernel, n, steps),
        out_shape=arrays((own, classes), (8, 128), (own, hid), (PARTS, rows, classes)),
        in_specs=[smem, smem, vmem, hbm, vmem, vmem, vmem],
        out_specs=[hbm, vmem, hbm, hbm],
        scratch_shapes=scratch,
        compiler_params=pltpu.CompilerParams(
            collective_id=0, has_side_effects=True, vmem_limit_bytes=56 * 1024 * 1024),
        name="step",
    )(block_index, block_counts, features, adjacency, labels[None, :], weight_in, weight_out)
    logits, loss, hidden_grad, grad_in, grad_out = pl.pallas_call(
        functools.partial(place, float(own * n)),
        out_shape=arrays((own, classes), (1, 1), (own, hid), (f_in, hid), (hid, classes)),
        in_specs=[hbm, smem, hbm, hbm],
        out_specs=[hbm, smem, hbm, hbm, hbm],
        scratch_shapes=[
            plain(own, classes), plain(own, hid), plain(PARTS, rows, classes),
            pltpu.SemaphoreType.DMA((2, 6 + hid // classes))],
        compiler_params=pltpu.CompilerParams(vmem_limit_bytes=63 * 1024 * 1024),
        name="place",
    )(logits, loss, hidden_grad, packed)
    return (logits, loss[0, 0], hidden_grad, grad_in, grad_out)


def solution(mesh):
    in_specs = (
        P("rows", None),
        P("rows", None, None, None),
        P("rows", None),
        P("rows"),
        P("rows"),
        P(),
        P(),
    )
    out_specs = (P("rows", None), P(), P("rows", None), P(), P())
    return jax.shard_map(
        functools.partial(per_device, mesh.shape["rows"]),
        mesh=mesh, in_specs=in_specs, out_specs=out_specs, check_vma=False,
    )
```

```python
import functools

import jax
import jax.numpy as jnp
from jax import lax
from jax.experimental import pallas as pl
from jax.experimental.pallas import tpu as pltpu
from jax.sharding import PartitionSpec as P

REACH = 2
F32 = jnp.float32
BF16 = jnp.bfloat16
MESH = pl.DeviceIdType.MESH
PARTS = 3
SMALLEST = 16
TOGETHER = 3


def split(value):
    high = value.astype(BF16)
    return high, (value - high.astype(F32)).astype(BF16)


def mm(a_high, a_low, b_high, b_low):
    def one(a, b):
        return jnp.dot(a, b, preferred_element_type=F32)

    return one(a_high, b_high) + (one(a_high, b_low) + one(a_low, b_high))


def mm_beside(a_high, a_low, b_both):
    width = b_both.shape[1] // 2
    wide = jnp.dot(a_high, b_both, preferred_element_type=F32)
    return wide[:, :width] + (wide[:, width:] + jnp.dot(a_low, b_both[:, :width], preferred_element_type=F32))


def chunks(total, size, body):
    def step(i, carry):
        body(pl.ds(pl.multiple_of(i * size, size), size))
        return carry

    lax.fori_loop(0, total // size, step, 0)


def plan(n, rows):
    bits = list(range(n.bit_length() - 1))
    cut = min(len(bits), (rows // SMALLEST).bit_length() - 1)
    parts = []
    for part in range(PARTS):
        near = bits[1:4]
        turn = part % max(1, len(near))
        order = bits[:1] + near[turn:] + near[:turn] + bits[4:]
        groups = [(bit,) for bit in order[: cut - TOGETHER]] + [tuple(order[cut - TOGETHER : cut])] + [(bit,) for bit in order[cut:]]
        length, offset, message, steps = rows, 0, 0, []
        for number, group in enumerate(groups):
            members = 1 << len(group)
            cuts = number < cut - TOGETHER + 1
            if cuts:
                length //= members
            steps.append((group, length, offset, message, cuts))
            offset += (members - 1) * length
            message += members - 1
        parts.append(steps)
    return parts, offset, message


def kernel(
    n, steps, index_ref, counts_ref, features, adjacency_hbm, labels, weight_in, weight_out,
    logits_out, loss_out, hidden_grad_out, packed_out,
    adjacency, far_features, band, band_high, band_low, turned_high, turned_low,
    near_high, near_low, win_high, win_low, wout_both, back_high, back_low,
    spread_high, spread_low, spread_t_high, spread_t_low, spread, hidden, slope, hid_high, hid_low, hid_t_high, hid_t_low,
    onehot_ref, near_z, z_both, logits_ref, grad_both, out_low, out_high, in_low, in_high, returned,
    ret_both, hidden_grad, acc, landing, full, loss_acc, loss_in,
    halo_send, halo_recv, part_send, part_recv, loss_send, loss_recv, local_sem,
):
    me = lax.axis_index("rows")
    own = features.shape[0]
    here, slots, block = adjacency.shape[:3]
    wide = 2 * REACH + 1
    hid = weight_in.shape[1]
    classes = weight_out.shape[1]
    has_low, has_high = me > 0, me < n - 1
    lower, upper = jnp.maximum(me - 1, 0), jnp.minimum(me + 1, n - 1)

    fetch = pltpu.make_async_copy(adjacency_hbm, adjacency, local_sem.at[0])
    fetch.start()

    def bit_of(bit):
        return lax.rem(lax.div(me, 1 << bit), 2)

    def member(group, delta):
        other, theirs, mine = me, 0, 0
        for position, bit in enumerate(group):
            weight = 1 << (len(group) - 1 - position)
            value = bit_of(bit)
            mine = mine + value * weight
            if delta & weight:
                other = other + (1 - 2 * value) * (1 << bit)
                theirs = theirs + (1 - value) * weight
            else:
                theirs = theirs + value * weight
        return other, theirs, mine

    partners = sorted({
        sum(1 << bit for position, bit in enumerate(step[0]) if delta & (1 << (len(step[0]) - 1 - position)))
        for part in steps for step in part for delta in range(1, 1 << len(step[0]))})
    barrier = pltpu.get_barrier_semaphore()
    for mask in partners:
        other = me
        for bit in range(n.bit_length() - 1):
            if mask >> bit & 1:
                other = other + (1 - 2 * bit_of(bit)) * (1 << bit)
        pl.semaphore_signal(barrier, inc=1, device_id=(other,), device_id_type=MESH)

    @pl.when(has_low)
    def _():
        pl.semaphore_signal(barrier, inc=1, device_id=(lower,), device_id_type=MESH)

    @pl.when(has_high)
    def _():
        pl.semaphore_signal(barrier, inc=1, device_id=(upper,), device_id_type=MESH)

    pl.semaphore_wait(barrier, len(partners) + jnp.where(has_low, 1, 0) + jnp.where(has_high, 1, 0))

    def rows_of(b):
        return slice(b * block, (b + 1) * block)

    class Halo:
        def __init__(self, slot, to_upper, from_lower, to_lower, from_upper):
            def copy(way, i, source, target, device):
                return pltpu.make_async_remote_copy(
                    src_ref=source.at[pl.ds(i * block, block)], dst_ref=target.at[pl.ds(i * block, block)],
                    send_sem=halo_send.at[slot, way, i], recv_sem=halo_recv.at[slot, way, i],
                    device_id=(device,), device_id_type=MESH)

            self.ups = [copy(0, i, to_upper, from_lower, upper) for i in range(here)]
            self.downs = [copy(1, i, to_lower, from_upper, lower) for i in range(here)]
            self.from_lower, self.from_upper = from_lower, from_upper

        def clear(self):
            @pl.when(jnp.logical_not(has_low))
            def _():
                self.from_lower[...] = jnp.zeros(self.from_lower.shape, F32)

            @pl.when(jnp.logical_not(has_high))
            def _():
                self.from_upper[...] = jnp.zeros(self.from_upper.shape, F32)

        def up(self, i):
            @pl.when(has_high)
            def _():
                self.ups[i].start()

        def down(self, i):
            @pl.when(has_low)
            def _():
                self.downs[i].start()

        def wait_lower(self, i):
            @pl.when(has_low)
            def _():
                self.ups[i].wait_recv()

        def wait_upper(self, i):
            @pl.when(has_high)
            def _():
                self.downs[i].wait_recv()

        def sent(self):
            @pl.when(has_high)
            def _():
                for copy in self.ups:
                    copy.wait_send()

            @pl.when(has_low)
            def _():
                for copy in self.downs:
                    copy.wait_send()

    first = Halo(0, features, far_features.at[0], features, far_features.at[1])
    for i in range(here):
        first.up(here - 1 - i)
        first.down(i)
    first.clear()

    win_high[...], win_low[...] = split(weight_in[...])
    wout_both[:, :classes], wout_both[:, classes:] = split(weight_out[...])
    back_high[...], back_low[...] = split(weight_out[...].T)
    middle = slice(own, 2 * own)
    near_high[middle, :], near_low[middle, :] = split(features[...])
    for b in range(here):
        lanes = lax.broadcasted_iota(jnp.int32, (classes, block), 0)
        onehot_ref[rows_of(b), :] = jnp.where(labels[:, rows_of(b)] == lanes, 1.0, 0.0).astype(F32).T
    fetch.wait()
    for b in range(here):
        weights = []
        for k in range(slots):
            relative = index_ref[b, k] - (me * here - REACH) - b
            used = k < counts_ref[b]
            weights.append([
                jnp.where(jnp.logical_and(used, relative == j), 1.0, 0.0).astype(F32) for j in range(wide)])

        def densify(rows, b=b, weights=weights):
            sums = [None] * wide
            for k in range(slots):
                tile = adjacency[b, k, rows, :]
                for j in range(wide):
                    term = weights[k][j] * tile
                    sums[j] = term if k == 0 else sums[j] + term
            for j in range(wide):
                columns = rows_of(j)
                high, low = split(sums[j])
                band[b, rows, columns] = sums[j]
                band_high[b, rows, columns] = high
                band_low[b, rows, columns] = low

        chunks(block, 32, densify)

    def propagate(total, high, low, b, first_block, last_block, fresh=False):
        first_block, last_block = max(first_block, b), min(last_block, b + wide - 1)
        if first_block > last_block:
            return
        columns = slice((first_block - b) * block, (last_block - b + 1) * block)
        window = slice(first_block * block, (last_block + 1) * block)
        if low is None:
            value = mm_beside(band_high[b, :, columns], band_low[b, :, columns], high[window, :])
        else:
            value = mm(band_high[b, :, columns], band_low[b, :, columns], high[window, :], low[window, :])
        total[rows_of(b), :] = value if fresh else total[rows_of(b), :] + value

    for b in range(here):
        propagate(spread, near_high, near_low, b, REACH, REACH + here - 1, fresh=True)

    def arrive_features(side, i):
        if side == 0:
            first.wait_lower(i)
        else:
            first.wait_upper(i)
        place = i if side == 0 else REACH + here + i
        near_high[rows_of(place), :], near_low[rows_of(place), :] = split(far_features[side, rows_of(i), :])
        for b in range(here):
            propagate(spread, near_high, near_low, b, place, place)

    second = Halo(
        1, near_z.at[pl.ds(own, own)], near_z.at[pl.ds(0, own)],
        near_z.at[pl.ds(own, own)], near_z.at[pl.ds(2 * own, own)])

    def forward(b):
        rows = rows_of(b)
        spread_high[rows, :], spread_low[rows, :] = split(spread[rows, :])
        slope[rows, :] = mm(spread_high[rows, :], spread_low[rows, :], win_high[...], win_low[...])

        def gelu(i, carry):
            part = pl.ds(pl.multiple_of(b * block + i * 32, 32), 32)
            x = slope[part, :]
            below = 0.5 * (1.0 + lax.erf(x * 0.7071067811865476))
            value = x * below
            hidden[part, :] = value
            hid_high[part, :], hid_low[part, :] = split(value)
            slope[part, :] = below + x * (jnp.exp(-0.5 * x * x) * 0.3989422804014327)
            return carry

        lax.fori_loop(0, block // 32, gelu, 0)
        near_z[own + b * block : own + (b + 1) * block, :] = mm_beside(
            hid_high[rows, :], hid_low[rows, :], wout_both[...])
        second.up(b)
        second.down(b)

    arrive_features(0, 1)
    arrive_features(1, 0)
    arrive_features(0, 0)
    forward(0)
    arrive_features(1, 1)
    forward(1)
    second.clear()

    z_both[middle, :classes], z_both[middle, classes:] = split(near_z[middle, :])
    for b in range(here):
        propagate(logits_ref, z_both, None, b, REACH, REACH + here - 1, fresh=True)
    for b in range(here):
        rows = rows_of(b)
        spread_t_high[:, rows], spread_t_low[:, rows] = split(spread[rows, :].T)
        for c in range(hid // block):
            hid_t_high[rows_of(c), rows], hid_t_low[rows_of(c), rows] = split(hidden[rows, rows_of(c)].T)
    for b in range(here):
        for j in range(wide):
            high, low = split(band[b, :, rows_of(j)].T)
            turned_high[b, rows_of(j), :] = high
            turned_low[b, rows_of(j), :] = low
    for i in range(here):
        second.wait_lower(i)
        second.wait_upper(i)
        for place in (i, REACH + here + i):
            z_both[rows_of(place), :classes], z_both[rows_of(place), classes:] = split(near_z[rows_of(place), :])
            for b in range(here):
                propagate(logits_ref, z_both, None, b, place, place)
    place_logits = pltpu.make_async_copy(logits_ref, logits_out, local_sem.at[0])
    place_logits.start()

    loss_acc[...] = jnp.zeros(loss_acc.shape, F32)
    third = Halo(2, out_high, in_low, out_low, in_high)

    def softmax(b):
        rows = rows_of(b)
        logits = logits_ref[rows, :]
        totals = jnp.log(jnp.sum(jnp.exp(logits), axis=1, keepdims=True))
        onehot = onehot_ref[rows, :]
        row_loss = totals - jnp.sum(onehot * logits, axis=1, keepdims=True)
        loss_acc[...] += jnp.broadcast_to(jnp.sum(row_loss, axis=0, keepdims=True), loss_acc.shape)
        grad_both[rows, :classes], grad_both[rows, classes:] = split(jnp.exp(logits - totals) - onehot)

    def bucket(place):
        total = None
        for b in range(here):
            if 0 <= place - b < wide:
                term = mm_beside(
                    turned_high[b, rows_of(place - b), :], turned_low[b, rows_of(place - b), :],
                    grad_both[rows_of(b), :])
                total = term if total is None else total + term
        return total

    softmax(0)
    out_low[rows_of(0), :] = bucket(0)
    third.down(0)
    softmax(1)
    for i in range(here):
        out_high[rows_of(i), :] = bucket(REACH + here + i)
        third.up(i)
        if i > 0:
            out_low[rows_of(i), :] = bucket(i)
            third.down(i)
    third.clear()
    for i in range(here):
        returned[rows_of(i), :] = bucket(REACH + i)

    lows = [0] * PARTS
    stages = [
        [(0, s) for s in range(len(part))] + [(1, s) for s in reversed(range(len(part))) if part[s][4]] for part in steps]
    reached = [0] * PARTS
    flying = [None] * PARTS

    def start_stage(part):
        phase, s = stages[part][reached[part]]
        group, length, offset, message, cuts = steps[part][s]
        low, copies = lows[part], []
        if phase == 1 and (reached[part] == 0 or stages[part][reached[part] - 1][0] == 0):
            rows = pl.ds(pl.multiple_of(low, SMALLEST), length)
            full[part, rows, :] = acc[part, rows, :]
        for delta in range(1, 1 << len(group)):
            other, theirs, mine = member(group, delta)
            if phase == 0:
                start = low + theirs * length if cuts else low
                source = acc.at[part, pl.ds(pl.multiple_of(start, SMALLEST), length)]
                target = landing.at[part, pl.ds(offset + (delta - 1) * length, length)]
            else:
                source = target = full.at[part, pl.ds(pl.multiple_of(low, SMALLEST), length)]
            copy = pltpu.make_async_remote_copy(
                src_ref=source, dst_ref=target, send_sem=part_send.at[phase, part, message + delta - 1],
                recv_sem=part_recv.at[phase, part, message + delta - 1], device_id=(other,), device_id_type=MESH)
            copy.start()
            copies.append(copy)
        if cuts:
            lows[part] = low + mine * length if phase == 0 else low - mine * length
        flying[part] = copies

    def finish_stage(part):
        phase, s = stages[part][reached[part]]
        group, length, offset, _, _ = steps[part][s]
        for copy in flying[part]:
            copy.wait()
        if phase == 0:
            rows = pl.ds(pl.multiple_of(lows[part], SMALLEST), length)
            total = acc[part, rows, :]
            for i in range(len(flying[part])):
                total = total + landing[part, pl.ds(offset + i * length, length), :]
            acc[part, rows, :] = total
        reached[part] += 1

    loss_flying = []

    def start_loss(s):
        group, _, _, message, _ = steps[0][s]
        loss_flying.clear()
        for delta in range(1, 1 << len(group)):
            other, _, _ = member(group, delta)
            place = message + delta - 1
            copy = pltpu.make_async_remote_copy(
                src_ref=loss_acc, dst_ref=loss_in.at[place], send_sem=loss_send.at[place], recv_sem=loss_recv.at[place],
                device_id=(other,), device_id_type=MESH)
            copy.start()
            loss_flying.append(copy)

    def finish_loss(s):
        for copy in loss_flying:
            copy.wait()
        total = loss_acc[...]
        for i in range(len(loss_flying)):
            total = total + loss_in[steps[0][s][3] + i]
        loss_acc[...] = total

    start_loss(0)
    values = [None] * 2
    for b in range(here):
        rows = rows_of(b)
        third.wait_lower(b)
        third.wait_upper(b)
        ret_both[rows, :classes], ret_both[rows, classes:] = split(returned[rows, :] + (in_low[rows, :] + in_high[rows, :]))
        value = mm_beside(hid_t_high[:, rows], hid_t_low[:, rows], ret_both[rows, :])
        acc[2] = value if b == 0 else acc[2] + value
        if b == here - 1:
            start_stage(2)
        hidden_grad[rows, :] = mm(ret_both[rows, :classes], ret_both[rows, classes:], back_high[...], back_low[...])

        def pre_grad(i, carry, b=b):
            part = pl.ds(pl.multiple_of(b * block + i * 32, 32), 32)
            hid_high[part, :], hid_low[part, :] = split(hidden_grad[part, :] * slope[part, :])
            return carry

        lax.fori_loop(0, block // 32, pre_grad, 0)
        if b == here - 1:
            place_hidden = pltpu.make_async_copy(hidden_grad, hidden_grad_out, local_sem.at[1])
            place_hidden.start()
            finish_stage(2)
            start_stage(2)
            finish_loss(0)
            start_loss(1)
        for part in range(2):
            columns = slice(part * hid // 2, (part + 1) * hid // 2)
            value = mm(spread_t_high[:, rows], spread_t_low[:, rows], hid_high[rows, columns], hid_low[rows, columns])
            for i in range(2):
                piece = value[:, i * classes : (i + 1) * classes]
                acc[part, rows_of(i), :] = piece if b == 0 else acc[part, rows_of(i), :] + piece
            if b == here - 1:
                start_stage(part)

    placing = []
    loss_step = 1
    while any(reached[part] < len(stages[part]) for part in range(PARTS)):
        for part in (2, 0, 1):
            if reached[part] == len(stages[part]):
                continue
            finish_stage(part)
            if reached[part] < len(stages[part]):
                start_stage(part)
            else:
                copy = pltpu.make_async_copy(full.at[part], packed_out.at[part], local_sem.at[2 + part])
                copy.start()
                placing.append(copy)
        if loss_step < len(steps[0]):
            finish_loss(loss_step)
            loss_step += 1
            if loss_step < len(steps[0]):
                start_loss(loss_step)
            else:
                loss_out[...] = loss_acc[...]
    for halo in (first, second, third):
        halo.sent()
    for copy in [place_logits, place_hidden] + placing:
        copy.wait()


def place(
    total, logits, loss, hidden_grad, packed, logits_out, loss_out, hidden_grad_out, grad_in_out, grad_out_out,
    logits_here, hidden_here, packed_here, sems,
):
    f_in, hid = grad_in_out.shape
    classes = logits.shape[1]
    quarter = hidden_grad.shape[0] // 4
    moves = []
    for i in range(4):
        rows = pl.ds(i * quarter, quarter)
        moves.append((hidden_grad.at[rows], hidden_here.at[rows], hidden_grad_out.at[rows]))
    for i in range(hid // classes):
        piece = (i // 2, pl.ds(i % 2 * f_in, f_in))
        moves.append((packed.at[piece], packed_here.at[piece], grad_in_out.at[:, pl.ds(i * classes, classes)]))
    moves.append((packed.at[2], packed_here.at[2], grad_out_out))
    moves.append((logits, logits_here, logits_out))
    fetches = [pltpu.make_async_copy(source, via, sems.at[0, i]) for i, (source, via, _) in enumerate(moves)]
    stores = [pltpu.make_async_copy(via, target, sems.at[1, i]) for i, (_, via, target) in enumerate(moves)]
    for copy in fetches:
        copy.start()
    loss_out[0, 0] = loss[0, 0] * (1.0 / total)
    for fetch, store in zip(fetches, stores):
        fetch.wait()
        store.start()
    for copy in stores:
        copy.wait()


def per_device(n, features, adjacency, block_index, block_counts, labels, weight_in, weight_out):
    own, f_in = features.shape
    here, _, block, _ = adjacency.shape
    hid, classes = weight_out.shape
    wide = 2 * REACH + 1
    rows = hid
    steps, landing, messages = plan(n, rows)

    def both(*shape):
        return [pltpu.VMEM(shape, BF16)] * 2

    def beside(length):
        return pltpu.VMEM((length, 2 * classes), BF16)

    def plain(*shape):
        return pltpu.VMEM(shape, F32)

    scratch = [
        plain(*adjacency.shape), plain(2, own, f_in), plain(here, block, wide * block), *both(here, block, wide * block),
        *both(here, wide * block, block), *both(3 * own, f_in), *both(f_in, hid), beside(hid),
        *both(classes, hid), *both(own, f_in), *both(f_in, own), plain(own, f_in), plain(own, hid), plain(own, hid),
        *both(own, hid), *both(hid, own), plain(own, classes), plain(3 * own, classes), beside(3 * own),
        plain(own, classes), beside(own),
        plain(own, classes), plain(own, classes), plain(own, classes), plain(own, classes), plain(own, classes),
        beside(own), plain(own, hid),
        plain(PARTS, rows, classes), plain(PARTS, landing, classes), plain(PARTS, rows, classes),
        plain(8, 128), plain(messages, 8, 128),
        pltpu.SemaphoreType.DMA((3, 2, here)), pltpu.SemaphoreType.DMA((3, 2, here)),
        pltpu.SemaphoreType.DMA((2, PARTS, messages)), pltpu.SemaphoreType.DMA((2, PARTS, messages)),
        pltpu.SemaphoreType.DMA((messages,)), pltpu.SemaphoreType.DMA((messages,)),
        pltpu.SemaphoreType.DMA((2 + PARTS,)),
    ]
    smem, vmem, hbm = (pl.BlockSpec(memory_space=space) for space in (pltpu.SMEM, pltpu.VMEM, pltpu.HBM))

    def arrays(*shapes):
        return [jax.ShapeDtypeStruct(shape, F32) for shape in shapes]

    logits, loss, hidden_grad, packed = pl.pallas_call(
        functools.partial(kernel, n, steps),
        out_shape=arrays((own, classes), (8, 128), (own, hid), (PARTS, rows, classes)),
        in_specs=[smem, smem, vmem, hbm, vmem, vmem, vmem],
        out_specs=[hbm, vmem, hbm, hbm],
        scratch_shapes=scratch,
        compiler_params=pltpu.CompilerParams(
            collective_id=0, has_side_effects=True, vmem_limit_bytes=56 * 1024 * 1024),
        name="step",
    )(block_index, block_counts, features, adjacency, labels[None, :], weight_in, weight_out)
    logits, loss, hidden_grad, grad_in, grad_out = pl.pallas_call(
        functools.partial(place, float(own * n)),
        out_shape=arrays((own, classes), (1, 1), (own, hid), (f_in, hid), (hid, classes)),
        in_specs=[hbm, smem, hbm, hbm],
        out_specs=[hbm, smem, hbm, hbm, hbm],
        scratch_shapes=[
            plain(own, classes), plain(own, hid), plain(PARTS, rows, classes),
            pltpu.SemaphoreType.DMA((2, 6 + hid // classes))],
        compiler_params=pltpu.CompilerParams(vmem_limit_bytes=63 * 1024 * 1024),
        name="place",
    )(logits, loss, hidden_grad, packed)
    return (logits, loss[0, 0], hidden_grad, grad_in, grad_out)


def solution(mesh):
    in_specs = (
        P("rows", None),
        P("rows", None, None, None),
        P("rows", None),
        P("rows"),
        P("rows"),
        P(),
        P(),
    )
    out_specs = (P("rows", None), P(), P("rows", None), P(), P())
    return jax.shard_map(
        functools.partial(per_device, mesh.shape["rows"]),
        mesh=mesh, in_specs=in_specs, out_specs=out_specs, check_vma=False,
    )
```
